32 devices in a mesh: tm: 4 (over z), space: 8 (over y, x, core).
Axes of the slice: x: 2, y: 2, z: 4, core: 2. Of those that a mesh axis runs over, the one named last changes fastest.
Arguments:
- states: float32 [4, 64, 64, 256], P('tm', 'space'), may hold values from -6 to 6
- conductivity: float32 [64, 64, 256], P('space'), may hold values from 0.4 to 1.6
Outputs:
- updated: float32 [4, 64, 64, 256], P('tm', 'space')
The draws below stay inside these ranges and needn't reach their ends.
All inputs are finite; a program needn't handle non-finite values.
Results may differ from the reference program's by a relative error of at most 0.0001.
Values sent between devices are 32-bit elements; how exact they have to be, the bound alone decides.
A program may use at most 64 MiB of HBM per device.

```python
import math
import jax
import jax.numpy as jnp
from jax import lax

NX = 64
NY = 256
FSTEPS = 4
NZ = 64
SLICES = 4


def levels(rng, extent, split, low, top_value):
    def one(axis_at, parts):
        draws = jax.random.uniform(jax.random.fold_in(jax.random.fold_in(rng, 6), axis_at), (parts,), jnp.float32, low / len(split), top_value / len(split))
        return jnp.repeat(jnp.exp(draws), extent[axis_at] // parts).reshape((-1,) + (1,) * (len(extent) - axis_at - 1))

    factor_of = one(*split[0])
    for cut in split[1:]:
        factor_of = factor_of * one(*cut)
    return factor_of


def centred(rng, shape, width, bound, cuts=(), dtype=jnp.bfloat16):
    result = jax.random.normal(rng, shape, jnp.float32) * width
    if len(cuts) > 0:
        result = levels(rng, shape, cuts, -0.22, 0.18) * result
    return jnp.clip(result, min=-bound, max=bound).astype(dtype)


def setup_inputs(seed: int = 0) -> dict:
    streams_of = jax.random.split(jax.random.key(seed), 3)
    states = centred(streams_of[0], (SLICES, NZ, NX, NY), 1.0, 6.0, ((0, 4), (1, 8)), jnp.float32)
    conductivity = jnp.clip(jnp.exp(math.log(1.6) - 1.3862944 * jax.random.uniform(streams_of[1], (NZ, NX, NY), jnp.float32) ** levels(streams_of[1], (NZ, NX, NY), ((0, 8),), -0.2, 0.2)), 0.4, 1.6)
    return {"states": states, "conductivity": conductivity}


fine_rate = 0.1
coarsen = 4


def axis_div(field, conduct, axis):
    count = field.shape[axis]
    upper = lax.slice_in_dim(field, 1, count, axis=axis)
    lower = lax.slice_in_dim(field, 0, count - 1, axis=axis)
    upper_c = lax.slice_in_dim(conduct, 1, count, axis=axis)
    lower_c = lax.slice_in_dim(conduct, 0, count - 1, axis=axis)
    flux = 0.5 * (upper_c + lower_c) * (upper - lower)
    widths = [(0, 0), (0, 0), (0, 0)]
    widths[axis] = (1, 1)
    padded = jnp.pad(flux, widths)
    return lax.slice_in_dim(padded, 1, count + 1, axis=axis) - lax.slice_in_dim(padded, 0, count, axis=axis)


def heat_step(field, conduct, step_rate):
    div_z = axis_div(field, conduct, 0)
    div_x = axis_div(field, conduct, 1)
    div_y = axis_div(field, conduct, 2)
    return field + step_rate * (div_z + div_x + div_y)


def restrict(field):
    planes, rows, cols = field.shape
    blocks = field.reshape(planes // coarsen, coarsen, rows // coarsen, coarsen, cols // coarsen, coarsen)
    return jnp.mean(blocks, axis=(1, 3, 5))


def prolong(coarse):
    return jnp.repeat(jnp.repeat(jnp.repeat(coarse, coarsen, axis=0), coarsen, axis=1), coarsen, axis=2)


def reference(states, conductivity):
    coarse_rate = fine_rate * FSTEPS / 16.0
    coarse_conduct = restrict(conductivity)
    slices = states.shape[0]
    fine_ends = []
    olds = []
    jumps = []
    for number in range(slices):
        field = states[number]
        for turn in range(FSTEPS):
            field = heat_step(field, conductivity, fine_rate)
        fine_ends.append(field)
        coarse_old = heat_step(restrict(states[number]), coarse_conduct, coarse_rate)
        olds.append(coarse_old)
        jumps.append(restrict(field) - coarse_old)
    coarse_now = restrict(states[0])
    outputs = []
    for number in range(slices):
        coarse_new = heat_step(coarse_now, coarse_conduct, coarse_rate)
        outputs.append(fine_ends[number] + prolong(coarse_new - olds[number]))
        coarse_now = coarse_new + jumps[number]
    return jnp.stack(outputs)
```

```python
import functools
import jax
import jax.numpy as jnp
from jax import lax
from jax.experimental import pallas as pl
from jax.experimental.pallas import tpu as pltpu
from jax.sharding import PartitionSpec as P

FSTEPS = 4
fine_rate = 0.1
coarsen = 4
LANES = 128
MESH = pl.DeviceIdType.MESH
HIGHEST = lax.Precision.HIGHEST


def group_matrix(shape, dim):
    fine = lax.broadcasted_iota(jnp.int32, shape, 1 - dim)
    coarse = lax.broadcasted_iota(jnp.int32, shape, dim)
    first = fine - coarse * coarsen
    return jnp.where((first >= 0) & (first < coarsen), 1.0, 0.0).astype(jnp.float32)


def dot(a, b):
    return jnp.dot(a, b, precision=HIGHEST, preferred_element_type=jnp.float32)


def kernel(
    slices, slabs, reach,
    states, conduct, out,
    field, cond, ax, ay, az,
    block, ext, first, jump, jumps,
    load_sem, fsend, frecv, csend, crecv, esend, erecv, ssend, srecv, jsend, jrecv,
):
    tm = lax.axis_index("tm")
    me = lax.axis_index("space")
    _, planes, rows, cols = states.shape
    crows, ccols = rows // coarsen, cols // coarsen
    cplanes = planes // coarsen
    pack = LANES // ccols
    far = reach(slices)
    blocks = 2 * far + 1
    offsets = [d for d in range(-far, far + 1) if d != 0]

    has_low = me > 0
    has_high = me < slabs - 1

    def inside(d):
        return (me + d >= 0) & (me + d < slabs)

    def later(delta):
        return tm + delta < slices

    load_v = pltpu.make_async_copy(states.at[0], field.at[0, pl.ds(1, planes)], load_sem.at[0])
    load_c = pltpu.make_async_copy(conduct, cond.at[pl.ds(1, planes)], load_sem.at[1])
    load_v.start()
    load_c.start()

    zero_plane = jnp.zeros((rows, cols), jnp.float32)

    @pl.when(jnp.logical_not(has_low))
    def _():
        cond[0] = zero_plane
        for k in range(FSTEPS):
            field[k, 0] = zero_plane

    @pl.when(jnp.logical_not(has_high))
    def _():
        cond[planes + 1] = zero_plane
        for k in range(FSTEPS):
            field[k, planes + 1] = zero_plane

    ext[...] = jnp.zeros(ext.shape, jnp.float32)
    jumps[...] = jnp.zeros(jumps.shape, jnp.float32)

    barrier = pltpu.get_barrier_semaphore()
    peers = [(0, d) for d in offsets]
    for delta in range(1, slices):
        for d in range(-reach(delta), reach(delta) + 1):
            peers += [(delta, d), (-delta, d)]
    count = jnp.int32(0)
    for dt, d in peers:
        there = inside(d) & (tm + dt >= 0) & (tm + dt < slices)

        @pl.when(there)
        def _(dt=dt, d=d):
            pl.semaphore_signal(barrier, inc=1, device_id=(tm + dt, me + d), device_id_type=MESH)

        count = count + there.astype(jnp.int32)
    pl.semaphore_wait(barrier, count)

    def halo(k, side):
        step = 1 if side == 0 else -1
        if k == 0:
            src = states.at[0, planes - 1 if side == 0 else 0]
        else:
            src = field.at[k, planes if side == 0 else 1]
        return pltpu.make_async_remote_copy(
            src_ref=src, dst_ref=field.at[k, 0 if side == 0 else planes + 1],
            send_sem=fsend.at[k, side], recv_sem=frecv.at[k, side],
            device_id=(tm, me + step), device_id_type=MESH,
        )

    def halo_c(side):
        step = 1 if side == 0 else -1
        return pltpu.make_async_remote_copy(
            src_ref=conduct.at[planes - 1 if side == 0 else 0],
            dst_ref=cond.at[0 if side == 0 else planes + 1],
            send_sem=csend.at[side], recv_sem=crecv.at[side],
            device_id=(tm, me + step), device_id_type=MESH,
        )

    sends_side = (has_high, has_low)
    hears_side = (has_low, has_high)

    for side in range(2):
        @pl.when(sends_side[side])
        def _(side=side):
            halo_c(side).start()
            halo(0, side).start()

    lane = lax.broadcasted_iota(jnp.int32, (crows, LANES), 1)
    gather_y = group_matrix((cols, LANES), 1)
    gather_x = group_matrix((cplanes * crows, cplanes * rows), 0)

    def restrict(ref, lead):
        sums = []
        for c in range(cplanes):
            total = ref[(*lead, 1 + c * coarsen)]
            for j in range(1, coarsen):
                total = total + ref[(*lead, 1 + c * coarsen + j)]
            sums.append(total)
        lanes = dot(jnp.concatenate(sums, axis=0), gather_y)
        return dot(gather_x, lanes) * (1.0 / coarsen**3)

    def packed(value):
        parts = []
        for g in range(cplanes // pack):
            total = None
            for j in range(pack):
                c = g * pack + j
                piece = value[c * crows : (c + 1) * crows]
                if j:
                    piece = pltpu.roll(piece, j * ccols, 1)
                total = piece if total is None else total + piece
            parts.append(total)
        return jnp.concatenate(parts, axis=0) if len(parts) > 1 else parts[0]

    def unpacked(values):
        parts = []
        for value in values:
            for g in range(cplanes // pack):
                piece = value[g * crows : (g + 1) * crows]
                for j in range(pack):
                    moved = pltpu.roll(piece, LANES - j * ccols, 1) if j else piece
                    parts.append(jnp.where(lane < ccols, moved, 0.0))
        return jnp.concatenate(parts, axis=0)

    def early(d):
        return pltpu.make_async_remote_copy(
            src_ref=block, dst_ref=ext.at[far - d],
            send_sem=esend.at[far + d], recv_sem=erecv.at[far - d],
            device_id=(tm, me + d), device_id_type=MESH,
        )

    load_v.wait()
    load_c.wait()
    block[0] = packed(restrict(field, (0,)))
    block[1] = packed(restrict(cond, ()))
    for d in offsets:
        @pl.when(inside(d))
        def _(d=d):
            early(d).start()
    ext[far] = block[...]

    half = 0.5 * fine_rate
    row_face = lax.broadcasted_iota(jnp.int32, (rows, cols), 0) < rows - 1
    col_face = lax.broadcasted_iota(jnp.int32, (rows, cols), 1) < cols - 1

    def faces(p, carry):
        c = cond[p]
        ax[p - 1] = jnp.where(row_face, half * (c + pltpu.roll(c, rows - 1, 0)), 0.0)
        ay[p - 1] = jnp.where(col_face, half * (c + pltpu.roll(c, cols - 1, 1)), 0.0)
        return carry

    def faces_z(p, carry):
        az[p] = half * (cond[p] + cond[p + 1])
        return carry

    lax.fori_loop(1, planes + 1, faces, 0)
    lax.fori_loop(1, planes, faces_z, 0)

    def advance(k, p):
        v = field[k, p]
        fx = ax[p - 1] * (pltpu.roll(v, rows - 1, 0) - v)
        fy = ay[p - 1] * (pltpu.roll(v, cols - 1, 1) - v)
        high = az[p] * (field[k, p + 1] - v)
        low = az[p - 1] * (v - field[k, p - 1])
        div = (high - low) + (fx - pltpu.roll(fx, 1, 0)) + (fy - pltpu.roll(fy, 1, 1))
        field[k + 1, p] = v + div

    def fine_step(k):
        for side in range(2):
            edge = 1 if side == 0 else planes

            @pl.when(hears_side[side])
            def _(side=side):
                if k == 0:
                    halo_c(side).wait_recv()
                halo(k, side).wait_recv()

            if k == 0:
                low_plane = 0 if side == 0 else planes
                scale = jnp.where(hears_side[side], half, 0.0)
                az[low_plane] = scale * (cond[low_plane] + cond[low_plane + 1])
            advance(k, edge)
            if k < FSTEPS - 1:
                @pl.when(sends_side[1 - side])
                def _(side=side):
                    halo(k + 1, 1 - side).start()

        def inner(p, carry):
            advance(k, p)
            return carry

        lax.fori_loop(2, planes, inner, 0)

    total_rows = blocks * cplanes * crows

    def coarse_faces():
        c = unpacked([ext[b, 1] for b in range(blocks)])
        half_c = 0.5 * fine_rate * FSTEPS / 16.0
        row = lax.broadcasted_iota(jnp.int32, (total_rows, LANES), 0)
        col = lax.broadcasted_iota(jnp.int32, (total_rows, LANES), 1)
        cx = jnp.where(row % crows < crows - 1, half_c * (c + pltpu.roll(c, total_rows - 1, 0)), 0.0)
        cy = jnp.where(col < ccols - 1, half_c * (c + pltpu.roll(c, LANES - 1, 1)), 0.0)
        ahead = row + (me - far) * (cplanes * crows)
        valid = (ahead >= 0) & (ahead < (slabs * cplanes - 1) * crows) & (row < total_rows - crows)
        cz = jnp.where(valid, half_c * (c + pltpu.roll(c, total_rows - crows, 0)), 0.0)
        return cx, cy, cz

    def propagate(w, coef):
        cx, cy, cz = coef
        fx = cx * (pltpu.roll(w, total_rows - 1, 0) - w)
        fy = cy * (pltpu.roll(w, LANES - 1, 1) - w)
        fz = cz * (pltpu.roll(w, total_rows - crows, 0) - w)
        div = (fz - pltpu.roll(fz, crows, 0)) + (fx - pltpu.roll(fx, 1, 0)) + (fy - pltpu.roll(fy, 1, 1))
        return w + div

    centre = slice(far * cplanes * crows, (far + 1) * cplanes * crows)

    def start_copy(delta):
        return pltpu.make_async_remote_copy(
            src_ref=first.at[0], dst_ref=first.at[1],
            send_sem=ssend.at[delta - 1], recv_sem=srecv,
            device_id=(tm + delta, me), device_id_type=MESH,
        )

    fine_step(0)

    for d in offsets:
        @pl.when(inside(d))
        def _(d=d):
            early(-d).wait_recv()
    for b in range(blocks):
        first[0, b] = ext[b, 0]
    for delta in range(1, slices):
        @pl.when((tm == 0) & (delta < slices))
        def _(delta=delta):
            start_copy(delta).start()

    fine_step(1)
    coef = coarse_faces()
    coarse_old = propagate(unpacked([first[0, b] for b in range(blocks)]), coef)[centre]
    fine_step(2)
    fine_step(3)

    jump[...] = packed(restrict(field, (FSTEPS,)) - coarse_old)

    def jump_copy(delta, d):
        at = (delta - 1) * blocks
        return pltpu.make_async_remote_copy(
            src_ref=jump, dst_ref=jumps.at[delta - 1, far - d],
            send_sem=jsend.at[at + far + d], recv_sem=jrecv.at[at + far - d],
            device_id=(tm + delta, me + d), device_id_type=MESH,
        )

    routes = [
        (delta, d)
        for delta in range(1, slices)
        for d in sorted(range(-reach(delta), reach(delta) + 1), key=lambda d: -abs(d))
    ]
    for delta, d in routes:
        @pl.when(later(delta) & inside(d))
        def _(delta=delta, d=d):
            jump_copy(delta, d).start()

    @pl.when(tm > 0)
    def _():
        start_copy(1).wait_recv()

    @pl.when(tm == 0)
    def _():
        first[1] = first[0]

    w = unpacked([first[1, b] for b in range(blocks)])
    for delta in range(slices - 1, 0, -1):
        for at, d in routes:
            if at == delta:
                @pl.when((tm >= delta) & inside(d))
                def _(delta=delta, d=d):
                    jump_copy(delta, -d).wait_recv()
        new = propagate(w, coef) + unpacked([jumps[delta - 1, b] for b in range(blocks)])
        w = jnp.where(tm >= delta, new, w)
    change = propagate(w, coef)[centre] - coarse_old

    spread_x = group_matrix((cplanes * rows, cplanes * crows), 1)
    spread_y = group_matrix((LANES, cols), 0)
    spread = dot(dot(spread_x, change), spread_y)
    stores = []
    for c in range(cplanes):
        piece = spread[c * rows : (c + 1) * rows]
        at = 1 + c * coarsen
        for j in range(coarsen):
            field[FSTEPS, at + j] = field[FSTEPS, at + j] + piece
        store = pltpu.make_async_copy(
            field.at[FSTEPS, pl.ds(at, coarsen)],
            out.at[0, pl.ds(c * coarsen, coarsen)],
            load_sem.at[2 + c],
        )
        store.start()
        stores.append(store)

    for side in range(2):
        @pl.when(sends_side[side])
        def _(side=side):
            halo_c(side).wait_send()
            for k in range(FSTEPS):
                halo(k, side).wait_send()
    for d in offsets:
        @pl.when(inside(d))
        def _(d=d):
            early(d).wait_send()
    for delta in range(1, slices):
        @pl.when(tm == 0)
        def _(delta=delta):
            start_copy(delta).wait_send()
    for delta, d in routes:
        @pl.when(later(delta) & inside(d))
        def _(delta=delta, d=d):
            jump_copy(delta, d).wait_send()
    for store in stores:
        store.wait()


def per_device(slices, slabs, states, conductivity):
    _, planes, rows, cols = states.shape
    cplanes, crows = planes // coarsen, rows // coarsen
    pack = LANES // (cols // coarsen)
    packed_rows = cplanes // pack * crows

    def reach(delta):
        return -(-delta // cplanes)

    far = reach(slices)
    blocks = 2 * far + 1
    f32 = jnp.float32
    dma = pltpu.SemaphoreType.DMA
    hops = max(slices - 1, 1)
    return pl.pallas_call(
        functools.partial(kernel, slices, slabs, reach),
        out_shape=jax.ShapeDtypeStruct(states.shape, f32),
        in_specs=[pl.BlockSpec(memory_space=pl.ANY)] * 2,
        out_specs=pl.BlockSpec(memory_space=pl.ANY),
        scratch_shapes=[
            pltpu.VMEM((FSTEPS + 1, planes + 2, rows, cols), f32),
            pltpu.VMEM((planes + 2, rows, cols), f32),
            pltpu.VMEM((planes, rows, cols), f32),
            pltpu.VMEM((planes, rows, cols), f32),
            pltpu.VMEM((planes + 1, rows, cols), f32),
            pltpu.VMEM((2, packed_rows, LANES), f32),
            pltpu.VMEM((blocks, 2, packed_rows, LANES), f32),
            pltpu.VMEM((2, blocks, packed_rows, LANES), f32),
            pltpu.VMEM((packed_rows, LANES), f32),
            pltpu.VMEM((hops, blocks, packed_rows, LANES), f32),
            dma((2 + cplanes,)),
            dma((FSTEPS, 2)),
            dma((FSTEPS, 2)),
            dma((2,)),
            dma((2,)),
            dma((blocks,)),
            dma((blocks,)),
            dma((hops,)),
            dma,
            dma((hops * blocks,)),
            dma((hops * blocks,)),
        ],
        compiler_params=pltpu.CompilerParams(
            collective_id=0, has_side_effects=True, vmem_limit_bytes=32 * 1024 * 1024
        ),
    )(states, conductivity)


def solution(mesh):
    in_specs = (P("tm", "space", None, None), P("space", None, None))
    out_specs = P("tm", "space", None, None)
    return jax.shard_map(
        functools.partial(per_device, mesh.shape["tm"], mesh.shape["space"]),
        mesh=mesh, in_specs=in_specs, out_specs=out_specs, check_vma=False,
    )
```

```python
import functools
import jax
import jax.numpy as jnp
from jax import lax
from jax.experimental import pallas as pl
from jax.experimental.pallas import tpu as pltpu
from jax.sharding import PartitionSpec as P

FSTEPS = 4
fine_rate = 0.1
coarsen = 4
LANES = 128
MESH = pl.DeviceIdType.MESH
HIGHEST = lax.Precision.HIGHEST


def group_matrix(shape, dim):
    fine = lax.broadcasted_iota(jnp.int32, shape, 1 - dim)
    coarse = lax.broadcasted_iota(jnp.int32, shape, dim)
    first = fine - coarse * coarsen
    return jnp.where((first >= 0) & (first < coarsen), 1.0, 0.0).astype(jnp.float32)


def dot(a, b):
    return jnp.dot(a, b, precision=HIGHEST, preferred_element_type=jnp.float32)


def kernel(
    slices, slabs, reach,
    states, conduct, out,
    field, cond, ax, ay, az,
    block, ext, first, jump, jumps,
    load_sem, fsend, frecv, csend, crecv, esend, erecv, ssend, srecv, jsend, jrecv, token,
):
    tm = lax.axis_index("tm")
    me = lax.axis_index("space")
    _, planes, rows, cols = states.shape
    crows, ccols = rows // coarsen, cols // coarsen
    cplanes = planes // coarsen
    pack = LANES // ccols
    far = reach(slices)
    blocks = 2 * far + 1
    offsets = [d for d in range(-far, far + 1) if d != 0]

    has_low = me > 0
    has_high = me < slabs - 1

    def inside(d):
        return (me + d >= 0) & (me + d < slabs)

    def later(delta):
        return tm + delta < slices

    load_v = pltpu.make_async_copy(states.at[0], field.at[0, pl.ds(1, planes)], load_sem.at[0])
    load_c = pltpu.make_async_copy(conduct, cond.at[pl.ds(1, planes)], load_sem.at[1])
    load_v.start()
    load_c.start()

    zero_plane = jnp.zeros((rows, cols), jnp.float32)

    @pl.when(jnp.logical_not(has_low))
    def _():
        cond[0] = zero_plane
        for k in range(FSTEPS):
            field[k, 0] = zero_plane

    @pl.when(jnp.logical_not(has_high))
    def _():
        cond[planes + 1] = zero_plane
        for k in range(FSTEPS):
            field[k, planes + 1] = zero_plane

    ext[...] = jnp.zeros(ext.shape, jnp.float32)
    jumps[...] = jnp.zeros(jumps.shape, jnp.float32)

    barrier = pltpu.get_barrier_semaphore()
    near = max(1, far - 1)
    peers = [(0, d) for d in range(-near, near + 1) if d != 0] + [(1, 0), (-1, 0)]
    count = jnp.int32(0)
    for dt, d in peers:
        there = inside(d) & (tm + dt >= 0) & (tm + dt < slices)

        @pl.when(there)
        def _(dt=dt, d=d):
            pl.semaphore_signal(barrier, inc=1, device_id=(tm + dt, me + d), device_id_type=MESH)

        count = count + there.astype(jnp.int32)
    pl.semaphore_wait(barrier, count)

    def halo(k, side):
        step = 1 if side == 0 else -1
        if k == 0:
            src = states.at[0, planes - 1 if side == 0 else 0]
        else:
            src = field.at[k, planes if side == 0 else 1]
        return pltpu.make_async_remote_copy(
            src_ref=src, dst_ref=field.at[k, 0 if side == 0 else planes + 1],
            send_sem=fsend.at[k, side], recv_sem=frecv.at[k, side],
            device_id=(tm, me + step), device_id_type=MESH,
        )

    def halo_c(side):
        step = 1 if side == 0 else -1
        return pltpu.make_async_remote_copy(
            src_ref=conduct.at[planes - 1 if side == 0 else 0],
            dst_ref=cond.at[0 if side == 0 else planes + 1],
            send_sem=csend.at[side], recv_sem=crecv.at[side],
            device_id=(tm, me + step), device_id_type=MESH,
        )

    sends_side = (has_high, has_low)
    hears_side = (has_low, has_high)

    for side in range(2):
        @pl.when(sends_side[side])
        def _(side=side):
            halo_c(side).start()
            halo(0, side).start()

    lane = lax.broadcasted_iota(jnp.int32, (crows, LANES), 1)
    gather_y = group_matrix((cols, LANES), 1)
    gather_x = group_matrix((cplanes * crows, cplanes * rows), 0)

    def restrict(ref, lead):
        sums = []
        for c in range(cplanes):
            total = ref[(*lead, 1 + c * coarsen)]
            for j in range(1, coarsen):
                total = total + ref[(*lead, 1 + c * coarsen + j)]
            sums.append(total)
        lanes = dot(jnp.concatenate(sums, axis=0), gather_y)
        return dot(gather_x, lanes) * (1.0 / coarsen**3)

    def packed(value):
        parts = []
        for g in range(cplanes // pack):
            total = None
            for j in range(pack):
                c = g * pack + j
                piece = value[c * crows : (c + 1) * crows]
                if j:
                    piece = pltpu.roll(piece, j * ccols, 1)
                total = piece if total is None else total + piece
            parts.append(total)
        return jnp.concatenate(parts, axis=0) if len(parts) > 1 else parts[0]

    def unpacked(values):
        parts = []
        for value in values:
            for g in range(cplanes // pack):
                piece = value[g * crows : (g + 1) * crows]
                for j in range(pack):
                    moved = pltpu.roll(piece, LANES - j * ccols, 1) if j else piece
                    parts.append(jnp.where(lane < ccols, moved, 0.0))
        return jnp.concatenate(parts, axis=0)

    def early(d):
        return pltpu.make_async_remote_copy(
            src_ref=block, dst_ref=ext.at[far - d],
            send_sem=esend.at[far + d], recv_sem=erecv.at[far - d],
            device_id=(tm, me + d), device_id_type=MESH,
        )

    load_v.wait()
    load_c.wait()
    block[0] = packed(restrict(field, (0,)))
    block[1] = packed(restrict(cond, ()))
    ext[far] = block[...]

    def early_send(distances):
        for d in distances:
            @pl.when(inside(d))
            def _(d=d):
                early(d).start()

    early_send([d for d in offsets if abs(d) <= near])

    half = 0.5 * fine_rate
    row_face = lax.broadcasted_iota(jnp.int32, (rows, cols), 0) < rows - 1
    col_face = lax.broadcasted_iota(jnp.int32, (rows, cols), 1) < cols - 1

    def faces(p, carry):
        c = cond[p]
        ax[p - 1] = jnp.where(row_face, half * (c + pltpu.roll(c, rows - 1, 0)), 0.0)
        ay[p - 1] = jnp.where(col_face, half * (c + pltpu.roll(c, cols - 1, 1)), 0.0)
        return carry

    def faces_z(p, carry):
        az[p] = half * (cond[p] + cond[p + 1])
        return carry

    lax.fori_loop(1, planes + 1, faces, 0)
    lax.fori_loop(1, planes, faces_z, 0)

    def advance(k, p):
        v = field[k, p]
        fx = ax[p - 1] * (pltpu.roll(v, rows - 1, 0) - v)
        fy = ay[p - 1] * (pltpu.roll(v, cols - 1, 1) - v)
        high = az[p] * (field[k, p + 1] - v)
        low = az[p - 1] * (v - field[k, p - 1])
        div = (high - low) + (fx - pltpu.roll(fx, 1, 0)) + (fy - pltpu.roll(fy, 1, 1))
        field[k + 1, p] = v + div

    def fine_step(k):
        for side in range(2):
            edge = 1 if side == 0 else planes

            @pl.when(hears_side[side])
            def _(side=side):
                if k == 0:
                    halo_c(side).wait_recv()
                halo(k, side).wait_recv()

            if k == 0:
                low_plane = 0 if side == 0 else planes
                scale = jnp.where(hears_side[side], half, 0.0)
                az[low_plane] = scale * (cond[low_plane] + cond[low_plane + 1])
            advance(k, edge)
            if k < FSTEPS - 1:
                @pl.when(sends_side[1 - side])
                def _(side=side):
                    halo(k + 1, 1 - side).start()

        def inner(p, carry):
            advance(k, p)
            return carry

        lax.fori_loop(2, planes, inner, 0)

    total_rows = blocks * cplanes * crows

    def coarse_faces():
        c = unpacked([ext[b, 1] for b in range(blocks)])
        half_c = 0.5 * fine_rate * FSTEPS / 16.0
        row = lax.broadcasted_iota(jnp.int32, (total_rows, LANES), 0)
        col = lax.broadcasted_iota(jnp.int32, (total_rows, LANES), 1)
        cx = jnp.where(row % crows < crows - 1, half_c * (c + pltpu.roll(c, total_rows - 1, 0)), 0.0)
        cy = jnp.where(col < ccols - 1, half_c * (c + pltpu.roll(c, LANES - 1, 1)), 0.0)
        ahead = row + (me - far) * (cplanes * crows)
        valid = (ahead >= 0) & (ahead < (slabs * cplanes - 1) * crows) & (row < total_rows - crows)
        cz = jnp.where(valid, half_c * (c + pltpu.roll(c, total_rows - crows, 0)), 0.0)
        return cx, cy, cz

    def propagate(w, coef):
        cx, cy, cz = coef
        fx = cx * (pltpu.roll(w, total_rows - 1, 0) - w)
        fy = cy * (pltpu.roll(w, LANES - 1, 1) - w)
        fz = cz * (pltpu.roll(w, total_rows - crows, 0) - w)
        div = (fz - pltpu.roll(fz, crows, 0)) + (fx - pltpu.roll(fx, 1, 0)) + (fy - pltpu.roll(fy, 1, 1))
        return w + div

    centre = slice(far * cplanes * crows, (far + 1) * cplanes * crows)

    def start_copy(delta):
        return pltpu.make_async_remote_copy(
            src_ref=first.at[0], dst_ref=first.at[1],
            send_sem=ssend.at[delta - 1], recv_sem=srecv,
            device_id=(tm + delta, me), device_id_type=MESH,
        )

    def pass_token(r):
        @pl.when((tm > 0) & (tm + r < slices))
        def _():
            pl.semaphore_signal(token.at[r], inc=1, device_id=(tm - 1, me), device_id_type=MESH)

    def take_token(r):
        @pl.when(tm + 1 + r < slices)
        def _():
            pl.semaphore_wait(token.at[r], 1)

    def send_start(delta):
        @pl.when(tm == 0)
        def _():
            start_copy(delta).start()

    fine_step(0)
    early_send([d for d in offsets if abs(d) > near])
    if slices > 1:
        pass_token(0)

    fine_step(1)
    for d in offsets:
        @pl.when(inside(d))
        def _(d=d):
            early(-d).wait_recv()
    for b in range(blocks):
        first[0, b] = ext[b, 0]
    for r in range(slices - 2):
        if r == 0:
            take_token(0)
            pass_token(1)
    if slices > 1:
        if slices == 2:
            take_token(0)
        send_start(1)
    coef = coarse_faces()
    coarse_old = propagate(unpacked([first[0, b] for b in range(blocks)]), coef)[centre]
    fine_step(2)
    for r in range(1, slices - 1):
        take_token(r)
        if r + 1 < slices - 1:
            pass_token(r + 1)
        if r < slices - 2:
            send_start(r + 1)
    fine_step(3)
    if slices > 2:
        send_start(slices - 1)

    jump[...] = packed(restrict(field, (FSTEPS,)) - coarse_old)

    def jump_copy(delta, d):
        at = (delta - 1) * blocks
        return pltpu.make_async_remote_copy(
            src_ref=jump, dst_ref=jumps.at[delta - 1, far - d],
            send_sem=jsend.at[at + far + d], recv_sem=jrecv.at[at + far - d],
            device_id=(tm + delta, me + d), device_id_type=MESH,
        )

    routes = [
        (delta, d)
        for delta in range(1, slices)
        for d in sorted(range(-reach(delta), reach(delta) + 1), key=lambda d: -abs(d))
    ]
    for delta, d in routes:
        @pl.when(later(delta) & inside(d))
        def _(delta=delta, d=d):
            jump_copy(delta, d).start()

    @pl.when(tm > 0)
    def _():
        start_copy(1).wait_recv()

    @pl.when(tm == 0)
    def _():
        first[1] = first[0]

    w = unpacked([first[1, b] for b in range(blocks)])
    for delta in range(slices - 1, 0, -1):
        for at, d in routes:
            if at == delta:
                @pl.when((tm >= delta) & inside(d))
                def _(delta=delta, d=d):
                    jump_copy(delta, -d).wait_recv()
        new = propagate(w, coef) + unpacked([jumps[delta - 1, b] for b in range(blocks)])
        w = jnp.where(tm >= delta, new, w)
    change = propagate(w, coef)[centre] - coarse_old

    spread_x = group_matrix((cplanes * rows, cplanes * crows), 1)
    spread_y = group_matrix((LANES, cols), 0)
    spread = dot(dot(spread_x, change), spread_y)
    stores = []
    for c in range(cplanes):
        piece = spread[c * rows : (c + 1) * rows]
        at = 1 + c * coarsen
        for j in range(coarsen):
            field[FSTEPS, at + j] = field[FSTEPS, at + j] + piece
        store = pltpu.make_async_copy(
            field.at[FSTEPS, pl.ds(at, coarsen)],
            out.at[0, pl.ds(c * coarsen, coarsen)],
            load_sem.at[2 + c],
        )
        store.start()
        stores.append(store)

    for side in range(2):
        @pl.when(sends_side[side])
        def _(side=side):
            halo_c(side).wait_send()
            for k in range(FSTEPS):
                halo(k, side).wait_send()
    for d in offsets:
        @pl.when(inside(d))
        def _(d=d):
            early(d).wait_send()
    for delta in range(1, slices):
        @pl.when(tm == 0)
        def _(delta=delta):
            start_copy(delta).wait_send()
    for delta, d in routes:
        @pl.when(later(delta) & inside(d))
        def _(delta=delta, d=d):
            jump_copy(delta, d).wait_send()
    for store in stores:
        store.wait()


def per_device(slices, slabs, states, conductivity):
    _, planes, rows, cols = states.shape
    cplanes, crows = planes // coarsen, rows // coarsen
    pack = LANES // (cols // coarsen)
    packed_rows = cplanes // pack * crows

    def reach(delta):
        return -(-delta // cplanes)

    far = reach(slices)
    blocks = 2 * far + 1
    f32 = jnp.float32
    dma = pltpu.SemaphoreType.DMA
    hops = max(slices - 1, 1)
    return pl.pallas_call(
        functools.partial(kernel, slices, slabs, reach),
        out_shape=jax.ShapeDtypeStruct(states.shape, f32),
        in_specs=[pl.BlockSpec(memory_space=pltpu.HBM)] * 2,
        out_specs=pl.BlockSpec(memory_space=pl.ANY),
        scratch_shapes=[
            pltpu.VMEM((FSTEPS + 1, planes + 2, rows, cols), f32),
            pltpu.VMEM((planes + 2, rows, cols), f32),
            pltpu.VMEM((planes, rows, cols), f32),
            pltpu.VMEM((planes, rows, cols), f32),
            pltpu.VMEM((planes + 1, rows, cols), f32),
            pltpu.VMEM((2, packed_rows, LANES), f32),
            pltpu.VMEM((blocks, 2, packed_rows, LANES), f32),
            pltpu.VMEM((2, blocks, packed_rows, LANES), f32),
            pltpu.VMEM((packed_rows, LANES), f32),
            pltpu.VMEM((hops, blocks, packed_rows, LANES), f32),
            dma((2 + cplanes,)),
            dma((FSTEPS, 2)),
            dma((FSTEPS, 2)),
            dma((2,)),
            dma((2,)),
            dma((blocks,)),
            dma((blocks,)),
            dma((hops,)),
            dma,
            dma((hops * blocks,)),
            dma((hops * blocks,)),
            pltpu.SemaphoreType.REGULAR((hops,)),
        ],
        compiler_params=pltpu.CompilerParams(
            collective_id=0, has_side_effects=True, vmem_limit_bytes=32 * 1024 * 1024
        ),
    )(states, conductivity)


def solution(mesh):
    in_specs = (P("tm", "space", None, None), P("space", None, None))
    out_specs = P("tm", "space", None, None)
    return jax.shard_map(
        functools.partial(per_device, mesh.shape["tm"], mesh.shape["space"]),
        mesh=mesh, in_specs=in_specs, out_specs=out_specs, check_vma=False,
    )
```

```python
import functools
import jax
import jax.numpy as jnp
from jax import lax
from jax.experimental import pallas as pl
from jax.experimental.pallas import tpu as pltpu
from jax.sharding import PartitionSpec as P

FSTEPS = 4
fine_rate = 0.1
coarsen = 4
LANES = 128
PARTS = 2
EDGE = 8
MESH = pl.DeviceIdType.MESH
HIGHEST = lax.Precision.HIGHEST


def group_matrix(shape, dim):
    fine = lax.broadcasted_iota(jnp.int32, shape, 1 - dim)
    coarse = lax.broadcasted_iota(jnp.int32, shape, dim)
    first = fine - coarse * coarsen
    return jnp.where((first >= 0) & (first < coarsen), 1.0, 0.0).astype(jnp.float32)


def dot(a, b):
    return jnp.dot(a, b, precision=HIGHEST, preferred_element_type=jnp.float32)


def kernel(
    slices, slabs, reach,
    states, conduct, out,
    field, cond, ax, ay, az,
    block, ext, first, jump, jumps,
    load_sem, fsend, frecv, csend, crecv, esend, erecv, ssend, srecv, jsend, jrecv, token,
):
    tm = lax.axis_index("tm")
    me = lax.axis_index("space")
    _, planes, rows, cols = states.shape
    crows, ccols = rows // coarsen, cols // coarsen
    cplanes = planes // coarsen
    pack = LANES // ccols
    far = reach(slices)
    blocks = 2 * far + 1
    offsets = [d for d in range(-far, far + 1) if d != 0]

    has_low = me > 0
    has_high = me < slabs - 1

    def inside(d):
        return (me + d >= 0) & (me + d < slabs)

    def later(delta):
        return tm + delta < slices

    load_v = pltpu.make_async_copy(states.at[0], field.at[0, pl.ds(1, planes)], load_sem.at[0])
    load_c = pltpu.make_async_copy(conduct, cond.at[pl.ds(1, planes)], load_sem.at[1])
    load_v.start()
    load_c.start()

    zero_plane = jnp.zeros((rows, cols), jnp.float32)

    @pl.when(jnp.logical_not(has_low))
    def _():
        cond[0] = zero_plane
        for k in range(FSTEPS):
            field[k, 0] = zero_plane

    @pl.when(jnp.logical_not(has_high))
    def _():
        cond[planes + 1] = zero_plane
        for k in range(FSTEPS):
            field[k, planes + 1] = zero_plane

    ext[...] = jnp.zeros(ext.shape, jnp.float32)
    jumps[...] = jnp.zeros(jumps.shape, jnp.float32)

    barrier = pltpu.get_barrier_semaphore()
    near = max(1, far - 1)
    peers = [(0, d) for d in range(-near, near + 1) if d != 0] + [(1, 0), (-1, 0)]
    count = jnp.int32(0)
    for dt, d in peers:
        there = inside(d) & (tm + dt >= 0) & (tm + dt < slices)

        @pl.when(there)
        def _(dt=dt, d=d):
            pl.semaphore_signal(barrier, inc=1, device_id=(tm + dt, me + d), device_id_type=MESH)

        count = count + there.astype(jnp.int32)
    pl.semaphore_wait(barrier, count)

    part = rows // PARTS

    def halo(k, side, q):
        step = 1 if side == 0 else -1
        at = pl.ds(q * part, part)
        if k == 0:
            src = states.at[0, planes - 1 if side == 0 else 0, at]
        else:
            src = field.at[k, planes if side == 0 else 1, at]
        return pltpu.make_async_remote_copy(
            src_ref=src, dst_ref=field.at[k, 0 if side == 0 else planes + 1, at],
            send_sem=fsend.at[k, side, q], recv_sem=frecv.at[k, side, q],
            device_id=(tm, me + step), device_id_type=MESH,
        )

    def halo_c(side):
        step = 1 if side == 0 else -1
        return pltpu.make_async_remote_copy(
            src_ref=conduct.at[planes - 1 if side == 0 else 0],
            dst_ref=cond.at[0 if side == 0 else planes + 1],
            send_sem=csend.at[side], recv_sem=crecv.at[side],
            device_id=(tm, me + step), device_id_type=MESH,
        )

    sends_side = (has_high, has_low)
    hears_side = (has_low, has_high)

    for side in range(2):
        @pl.when(sends_side[side])
        def _(side=side):
            halo_c(side).start()
            for q in range(PARTS):
                halo(0, side, q).start()

    lane = lax.broadcasted_iota(jnp.int32, (crows, LANES), 1)
    gather_y = group_matrix((cols, LANES), 1)
    gather_x = group_matrix((cplanes * crows, cplanes * rows), 0)

    def restrict(ref, lead):
        sums = []
        for c in range(cplanes):
            total = ref[(*lead, 1 + c * coarsen)]
            for j in range(1, coarsen):
                total = total + ref[(*lead, 1 + c * coarsen + j)]
            sums.append(total)
        lanes = dot(jnp.concatenate(sums, axis=0), gather_y)
        return dot(gather_x, lanes) * (1.0 / coarsen**3)

    def packed(value):
        parts = []
        for g in range(cplanes // pack):
            total = None
            for j in range(pack):
                c = g * pack + j
                piece = value[c * crows : (c + 1) * crows]
                if j:
                    piece = pltpu.roll(piece, j * ccols, 1)
                total = piece if total is None else total + piece
            parts.append(total)
        return jnp.concatenate(parts, axis=0) if len(parts) > 1 else parts[0]

    def unpacked(values):
        parts = []
        for value in values:
            for g in range(cplanes // pack):
                piece = value[g * crows : (g + 1) * crows]
                for j in range(pack):
                    moved = pltpu.roll(piece, LANES - j * ccols, 1) if j else piece
                    parts.append(jnp.where(lane < ccols, moved, 0.0))
        return jnp.concatenate(parts, axis=0)

    def early(d):
        return pltpu.make_async_remote_copy(
            src_ref=block, dst_ref=ext.at[far - d],
            send_sem=esend.at[far + d], recv_sem=erecv.at[far - d],
            device_id=(tm, me + d), device_id_type=MESH,
        )

    load_v.wait()
    load_c.wait()
    block[0] = packed(restrict(field, (0,)))
    block[1] = packed(restrict(cond, ()))
    ext[far] = block[...]

    def early_send(distances):
        for d in distances:
            @pl.when(inside(d))
            def _(d=d):
                early(d).start()

    early_send([d for d in offsets if abs(d) <= near])

    half = 0.5 * fine_rate
    row_face = lax.broadcasted_iota(jnp.int32, (rows, cols), 0) < rows - 1
    col_face = lax.broadcasted_iota(jnp.int32, (rows, cols), 1) < cols - 1

    def faces(p, carry):
        c = cond[p]
        ax[p - 1] = jnp.where(row_face, half * (c + pltpu.roll(c, rows - 1, 0)), 0.0)
        ay[p - 1] = jnp.where(col_face, half * (c + pltpu.roll(c, cols - 1, 1)), 0.0)
        return carry

    def faces_z(p, carry):
        az[p] = half * (cond[p] + cond[p + 1])
        return carry

    lax.fori_loop(1, planes + 1, faces, 0)
    lax.fori_loop(1, planes, faces_z, 0)

    def advance(k, p):
        v = field[k, p]
        fx = ax[p - 1] * (pltpu.roll(v, rows - 1, 0) - v)
        fy = ay[p - 1] * (pltpu.roll(v, cols - 1, 1) - v)
        high = az[p] * (field[k, p + 1] - v)
        low = az[p - 1] * (v - field[k, p - 1])
        div = (high - low) + (fx - pltpu.roll(fx, 1, 0)) + (fy - pltpu.roll(fy, 1, 1))
        field[k + 1, p] = v + div

    def advance_part(k, p, q):
        start, stop = q * part, (q + 1) * part
        low_row, high_row = max(start - EDGE, 0), min(stop + EDGE, rows)
        size = high_row - low_row
        mine = slice(start - low_row, stop - low_row)
        window = field[k, p, low_row:high_row]
        inner_face = lax.broadcasted_iota(jnp.int32, (size, cols), 0) < size - 1
        fx = jnp.where(inner_face, ax[p - 1, low_row:high_row] * (pltpu.roll(window, size - 1, 0) - window), 0.0)
        div_x = (fx - pltpu.roll(fx, 1, 0))[mine]
        v = window[mine]
        fy = ay[p - 1, start:stop] * (pltpu.roll(v, cols - 1, 1) - v)
        high = az[p, start:stop] * (field[k, p + 1, start:stop] - v)
        low = az[p - 1, start:stop] * (v - field[k, p - 1, start:stop])
        div = (high - low) + div_x + (fy - pltpu.roll(fy, 1, 1))
        field[k + 1, p, start:stop] = v + div

    def inner_planes(k):
        def inner(p, carry):
            advance(k, p)
            return carry

        lax.fori_loop(2, planes, inner, 0)

    def fine_step(k):
        if k == FSTEPS - 1:
            inner_planes(k)
        for q in range(PARTS):
            for side in range(2):
                edge = 1 if side == 0 else planes

                @pl.when(hears_side[side])
                def _(side=side):
                    if k == 0 and q == 0:
                        halo_c(side).wait_recv()
                    halo(k, side, q).wait_recv()

                if k == 0 and q == 0:
                    low_plane = 0 if side == 0 else planes
                    scale = jnp.where(hears_side[side], half, 0.0)
                    az[low_plane] = scale * (cond[low_plane] + cond[low_plane + 1])
                advance_part(k, edge, q)
                if k < FSTEPS - 1:
                    @pl.when(sends_side[1 - side])
                    def _(side=side):
                        halo(k + 1, 1 - side, q).start()

        if k < FSTEPS - 1:
            inner_planes(k)

    total_rows = blocks * cplanes * crows

    def coarse_faces():
        c = unpacked([ext[b, 1] for b in range(blocks)])
        half_c = 0.5 * fine_rate * FSTEPS / 16.0
        row = lax.broadcasted_iota(jnp.int32, (total_rows, LANES), 0)
        col = lax.broadcasted_iota(jnp.int32, (total_rows, LANES), 1)
        cx = jnp.where(row % crows < crows - 1, half_c * (c + pltpu.roll(c, total_rows - 1, 0)), 0.0)
        cy = jnp.where(col < ccols - 1, half_c * (c + pltpu.roll(c, LANES - 1, 1)), 0.0)
        ahead = row + (me - far) * (cplanes * crows)
        valid = (ahead >= 0) & (ahead < (slabs * cplanes - 1) * crows) & (row < total_rows - crows)
        cz = jnp.where(valid, half_c * (c + pltpu.roll(c, total_rows - crows, 0)), 0.0)
        return cx, cy, cz

    def propagate(w, coef):
        cx, cy, cz = coef
        fx = cx * (pltpu.roll(w, total_rows - 1, 0) - w)
        fy = cy * (pltpu.roll(w, LANES - 1, 1) - w)
        fz = cz * (pltpu.roll(w, total_rows - crows, 0) - w)
        div = (fz - pltpu.roll(fz, crows, 0)) + (fx - pltpu.roll(fx, 1, 0)) + (fy - pltpu.roll(fy, 1, 1))
        return w + div

    centre = slice(far * cplanes * crows, (far + 1) * cplanes * crows)

    def start_copy(delta):
        return pltpu.make_async_remote_copy(
            src_ref=first.at[0], dst_ref=first.at[1],
            send_sem=ssend.at[delta - 1], recv_sem=srecv,
            device_id=(tm + delta, me), device_id_type=MESH,
        )

    def pass_token(r):
        @pl.when((tm > 0) & (tm + r < slices))
        def _():
            pl.semaphore_signal(token.at[r], inc=1, device_id=(tm - 1, me), device_id_type=MESH)

    def take_token(r):
        @pl.when(tm + 1 + r < slices)
        def _():
            pl.semaphore_wait(token.at[r], 1)

    def send_start(delta):
        @pl.when(tm == 0)
        def _():
            start_copy(delta).start()

    fine_step(0)
    early_send([d for d in offsets if abs(d) > near])
    if slices > 1:
        pass_token(0)

    fine_step(1)
    for d in offsets:
        @pl.when(inside(d))
        def _(d=d):
            early(-d).wait_recv()
    for b in range(blocks):
        first[0, b] = ext[b, 0]
    for r in range(slices - 2):
        if r == 0:
            take_token(0)
            pass_token(1)
    if slices > 1:
        if slices == 2:
            take_token(0)
        send_start(1)
    coef = coarse_faces()
    coarse_old = propagate(unpacked([first[0, b] for b in range(blocks)]), coef)[centre]
    fine_step(2)
    for r in range(1, slices - 1):
        take_token(r)
        if r + 1 < slices - 1:
            pass_token(r + 1)
        if r < slices - 2:
            send_start(r + 1)
    fine_step(3)
    if slices > 2:
        send_start(slices - 1)

    jump[...] = packed(restrict(field, (FSTEPS,)) - coarse_old)

    def jump_copy(delta, d):
        at = (delta - 1) * blocks
        return pltpu.make_async_remote_copy(
            src_ref=jump, dst_ref=jumps.at[delta - 1, far - d],
            send_sem=jsend.at[at + far + d], recv_sem=jrecv.at[at + far - d],
            device_id=(tm + delta, me + d), device_id_type=MESH,
        )

    routes = [
        (delta, d)
        for delta in range(1, slices)
        for d in sorted(range(-reach(delta), reach(delta) + 1), key=lambda d: -abs(d))
    ]
    for delta, d in routes:
        @pl.when(later(delta) & inside(d))
        def _(delta=delta, d=d):
            jump_copy(delta, d).start()

    @pl.when(tm > 0)
    def _():
        start_copy(1).wait_recv()

    @pl.when(tm == 0)
    def _():
        first[1] = first[0]

    w = unpacked([first[1, b] for b in range(blocks)])
    for delta in range(slices - 1, 0, -1):
        for at, d in routes:
            if at == delta:
                @pl.when((tm >= delta) & inside(d))
                def _(delta=delta, d=d):
                    jump_copy(delta, -d).wait_recv()
        new = propagate(w, coef) + unpacked([jumps[delta - 1, b] for b in range(blocks)])
        w = jnp.where(tm >= delta, new, w)
    change = propagate(w, coef)[centre] - coarse_old

    spread_x = group_matrix((cplanes * rows, cplanes * crows), 1)
    spread_y = group_matrix((LANES, cols), 0)
    spread = dot(dot(spread_x, change), spread_y)
    stores = []
    for c in range(cplanes):
        piece = spread[c * rows : (c + 1) * rows]
        at = 1 + c * coarsen
        for j in range(coarsen):
            field[FSTEPS, at + j] = field[FSTEPS, at + j] + piece
        store = pltpu.make_async_copy(
            field.at[FSTEPS, pl.ds(at, coarsen)],
            out.at[0, pl.ds(c * coarsen, coarsen)],
            load_sem.at[2 + c],
        )
        store.start()
        stores.append(store)

    for side in range(2):
        @pl.when(sends_side[side])
        def _(side=side):
            halo_c(side).wait_send()
            for k in range(FSTEPS):
                for q in range(PARTS):
                    halo(k, side, q).wait_send()
    for d in offsets:
        @pl.when(inside(d))
        def _(d=d):
            early(d).wait_send()
    for delta in range(1, slices):
        @pl.when(tm == 0)
        def _(delta=delta):
            start_copy(delta).wait_send()
    for delta, d in routes:
        @pl.when(later(delta) & inside(d))
        def _(delta=delta, d=d):
            jump_copy(delta, d).wait_send()
    for store in stores:
        store.wait()


def per_device(slices, slabs, states, conductivity):
    _, planes, rows, cols = states.shape
    cplanes, crows = planes // coarsen, rows // coarsen
    pack = LANES // (cols // coarsen)
    packed_rows = cplanes // pack * crows

    def reach(delta):
        return -(-delta // cplanes)

    far = reach(slices)
    blocks = 2 * far + 1
    f32 = jnp.float32
    dma = pltpu.SemaphoreType.DMA
    hops = max(slices - 1, 1)
    return pl.pallas_call(
        functools.partial(kernel, slices, slabs, reach),
        out_shape=jax.ShapeDtypeStruct(states.shape, f32),
        in_specs=[pl.BlockSpec(memory_space=pltpu.HBM)] * 2,
        out_specs=pl.BlockSpec(memory_space=pl.ANY),
        scratch_shapes=[
            pltpu.VMEM((FSTEPS + 1, planes + 2, rows, cols), f32),
            pltpu.VMEM((planes + 2, rows, cols), f32),
            pltpu.VMEM((planes, rows, cols), f32),
            pltpu.VMEM((planes, rows, cols), f32),
            pltpu.VMEM((planes + 1, rows, cols), f32),
            pltpu.VMEM((2, packed_rows, LANES), f32),
            pltpu.VMEM((blocks, 2, packed_rows, LANES), f32),
            pltpu.VMEM((2, blocks, packed_rows, LANES), f32),
            pltpu.VMEM((packed_rows, LANES), f32),
            pltpu.VMEM((hops, blocks, packed_rows, LANES), f32),
            dma((2 + cplanes,)),
            dma((FSTEPS, 2, PARTS)),
            dma((FSTEPS, 2, PARTS)),
            dma((2,)),
            dma((2,)),
            dma((blocks,)),
            dma((blocks,)),
            dma((hops,)),
            dma,
            dma((hops * blocks,)),
            dma((hops * blocks,)),
            pltpu.SemaphoreType.REGULAR((hops,)),
        ],
        compiler_params=pltpu.CompilerParams(
            collective_id=0, has_side_effects=True, vmem_limit_bytes=32 * 1024 * 1024
        ),
    )(states, conductivity)


def solution(mesh):
    in_specs = (P("tm", "space", None, None), P("space", None, None))
    out_specs = P("tm", "space", None, None)
    return jax.shard_map(
        functools.partial(per_device, mesh.shape["tm"], mesh.shape["space"]),
        mesh=mesh, in_specs=in_specs, out_specs=out_specs, check_vma=False,
    )
```

```python
import functools
import jax
import jax.numpy as jnp
from jax import lax
from jax.experimental import pallas as pl
from jax.experimental.pallas import tpu as pltpu
from jax.sharding import PartitionSpec as P

FSTEPS = 4
fine_rate = 0.1
coarsen = 4
LANES = 128
PARTS = 2
EDGE = 8
MESH = pl.DeviceIdType.MESH


def group_matrix(shape, dim):
    fine = lax.broadcasted_iota(jnp.int32, shape, 1 - dim)
    coarse = lax.broadcasted_iota(jnp.int32, shape, dim)
    first = fine - coarse * coarsen
    return jnp.where((first >= 0) & (first < coarsen), 1.0, 0.0).astype(jnp.float32)


def terms(a):
    parts = []
    for _ in range(3):
        parts.append(a.astype(jnp.bfloat16))
        a = a - parts[-1].astype(jnp.float32)
    return parts


def dot_right(a, ones):
    ones = ones.astype(jnp.bfloat16)
    return sum(jnp.dot(t, ones, preferred_element_type=jnp.float32) for t in terms(a)[::-1])


def dot_left(ones, b):
    ones = ones.astype(jnp.bfloat16)
    return sum(jnp.dot(ones, t, preferred_element_type=jnp.float32) for t in terms(b)[::-1])


def kernel(
    slices, slabs, reach,
    states, conduct, out,
    field, cond, ax, ay, az,
    block, ext, first, jump, jumps,
    load_sem, fsend, frecv, csend, crecv, esend, erecv, ssend, srecv, jsend, jrecv, token,
):
    tm = lax.axis_index("tm")
    me = lax.axis_index("space")
    _, planes, rows, cols = states.shape
    crows, ccols = rows // coarsen, cols // coarsen
    cplanes = planes // coarsen
    pack = LANES // ccols
    far = reach(slices)
    blocks = 2 * far + 1
    offsets = [d for d in range(-far, far + 1) if d != 0]

    has_low = me > 0
    has_high = me < slabs - 1

    def inside(d):
        return (me + d >= 0) & (me + d < slabs)

    def later(delta):
        return tm + delta < slices

    load_v = pltpu.make_async_copy(states.at[0], field.at[0, pl.ds(1, planes)], load_sem.at[0])
    load_c = pltpu.make_async_copy(conduct, cond.at[pl.ds(1, planes)], load_sem.at[1])
    load_v.start()
    load_c.start()

    zero_plane = jnp.zeros((rows, cols), jnp.float32)

    @pl.when(jnp.logical_not(has_low))
    def _():
        cond[0] = zero_plane
        for k in range(FSTEPS):
            field[k, 0] = zero_plane

    @pl.when(jnp.logical_not(has_high))
    def _():
        cond[planes + 1] = zero_plane
        for k in range(FSTEPS):
            field[k, planes + 1] = zero_plane

    ext[...] = jnp.zeros(ext.shape, jnp.float32)
    jumps[...] = jnp.zeros(jumps.shape, jnp.float32)

    barrier = pltpu.get_barrier_semaphore()
    near = max(1, far - 1)
    peers = [(0, d) for d in range(-near, near + 1) if d != 0] + [(1, 0), (-1, 0)]
    count = jnp.int32(0)
    for dt, d in peers:
        there = inside(d) & (tm + dt >= 0) & (tm + dt < slices)

        @pl.when(there)
        def _(dt=dt, d=d):
            pl.semaphore_signal(barrier, inc=1, device_id=(tm + dt, me + d), device_id_type=MESH)

        count = count + there.astype(jnp.int32)
    pl.semaphore_wait(barrier, count)

    part = rows // PARTS

    def halo(k, side, q):
        step = 1 if side == 0 else -1
        at = pl.ds(q * part, part)
        if k == 0:
            src = states.at[0, planes - 1 if side == 0 else 0, at]
        else:
            src = field.at[k, planes if side == 0 else 1, at]
        return pltpu.make_async_remote_copy(
            src_ref=src, dst_ref=field.at[k, 0 if side == 0 else planes + 1, at],
            send_sem=fsend.at[k, side, q], recv_sem=frecv.at[k, side, q],
            device_id=(tm, me + step), device_id_type=MESH,
        )

    def halo_c(side, q):
        step = 1 if side == 0 else -1
        at = pl.ds(q * part, part)
        return pltpu.make_async_remote_copy(
            src_ref=conduct.at[planes - 1 if side == 0 else 0, at],
            dst_ref=cond.at[0 if side == 0 else planes + 1, at],
            send_sem=csend.at[side, q], recv_sem=crecv.at[side, q],
            device_id=(tm, me + step), device_id_type=MESH,
        )

    sends_side = (has_high, has_low)
    hears_side = (has_low, has_high)

    for side in range(2):
        @pl.when(sends_side[side])
        def _(side=side):
            for q in range(PARTS):
                halo_c(side, q).start()
                halo(0, side, q).start()

    lane = lax.broadcasted_iota(jnp.int32, (crows, LANES), 1)
    gather_y = group_matrix((cols, LANES), 1)
    gather_x = group_matrix((cplanes * crows, cplanes * rows), 0)

    def restrict(ref, lead):
        sums = []
        for c in range(cplanes):
            total = ref[(*lead, 1 + c * coarsen)]
            for j in range(1, coarsen):
                total = total + ref[(*lead, 1 + c * coarsen + j)]
            sums.append(total)
        lanes = dot_right(jnp.concatenate(sums, axis=0), gather_y)
        return dot_left(gather_x, lanes) * (1.0 / coarsen**3)

    def packed(value):
        parts = []
        for g in range(cplanes // pack):
            total = None
            for j in range(pack):
                c = g * pack + j
                piece = value[c * crows : (c + 1) * crows]
                if j:
                    piece = pltpu.roll(piece, j * ccols, 1)
                total = piece if total is None else total + piece
            parts.append(total)
        return jnp.concatenate(parts, axis=0) if len(parts) > 1 else parts[0]

    def unpacked(values):
        parts = []
        for value in values:
            for g in range(cplanes // pack):
                piece = value[g * crows : (g + 1) * crows]
                for j in range(pack):
                    moved = pltpu.roll(piece, LANES - j * ccols, 1) if j else piece
                    parts.append(jnp.where(lane < ccols, moved, 0.0))
        return jnp.concatenate(parts, axis=0)

    def early(d):
        return pltpu.make_async_remote_copy(
            src_ref=block, dst_ref=ext.at[far - d],
            send_sem=esend.at[far + d], recv_sem=erecv.at[far - d],
            device_id=(tm, me + d), device_id_type=MESH,
        )

    load_v.wait()
    load_c.wait()
    block[0] = packed(restrict(field, (0,)))
    block[1] = packed(restrict(cond, ()))
    ext[far] = block[...]

    def early_send(distances):
        for d in distances:
            @pl.when(inside(d))
            def _(d=d):
                early(d).start()


    half = 0.5 * fine_rate
    row_face = lax.broadcasted_iota(jnp.int32, (rows, cols), 0) < rows - 1
    col_face = lax.broadcasted_iota(jnp.int32, (rows, cols), 1) < cols - 1

    def faces(p, carry):
        c = cond[p]
        ax[p - 1] = jnp.where(row_face, half * (c + pltpu.roll(c, rows - 1, 0)), 0.0)
        ay[p - 1] = jnp.where(col_face, half * (c + pltpu.roll(c, cols - 1, 1)), 0.0)
        return carry

    def faces_z(p, carry):
        az[p] = half * (cond[p] + cond[p + 1])
        return carry

    lax.fori_loop(1, planes + 1, faces, 0)
    lax.fori_loop(1, planes, faces_z, 0)

    def advance(k, p):
        v = field[k, p]
        fx = ax[p - 1] * (pltpu.roll(v, rows - 1, 0) - v)
        fy = ay[p - 1] * (pltpu.roll(v, cols - 1, 1) - v)
        high = az[p] * (field[k, p + 1] - v)
        low = az[p - 1] * (v - field[k, p - 1])
        div = (high - low) + (fx - pltpu.roll(fx, 1, 0)) + (fy - pltpu.roll(fy, 1, 1))
        field[k + 1, p] = v + div

    def advance_part(k, p, q):
        start, stop = q * part, (q + 1) * part
        low_row, high_row = max(start - EDGE, 0), min(stop + EDGE, rows)
        size = high_row - low_row
        mine = slice(start - low_row, stop - low_row)
        window = field[k, p, low_row:high_row]
        inner_face = lax.broadcasted_iota(jnp.int32, (size, cols), 0) < size - 1
        fx = jnp.where(inner_face, ax[p - 1, low_row:high_row] * (pltpu.roll(window, size - 1, 0) - window), 0.0)
        div_x = (fx - pltpu.roll(fx, 1, 0))[mine]
        v = window[mine]
        fy = ay[p - 1, start:stop] * (pltpu.roll(v, cols - 1, 1) - v)
        high = az[p, start:stop] * (field[k, p + 1, start:stop] - v)
        low = az[p - 1, start:stop] * (v - field[k, p - 1, start:stop])
        div = (high - low) + div_x + (fy - pltpu.roll(fy, 1, 1))
        field[k + 1, p, start:stop] = v + div

    def inner_planes(k):
        def inner(p, carry):
            advance(k, p)
            return carry

        lax.fori_loop(2, planes, inner, 0)

    def fine_step(k):
        if k == FSTEPS - 1:
            inner_planes(k)
        for q in range(PARTS):
            for side in range(2):
                edge = 1 if side == 0 else planes

                @pl.when(hears_side[side])
                def _(side=side):
                    if k == 0:
                        halo_c(side, q).wait_recv()
                    halo(k, side, q).wait_recv()

                if k == 0:
                    low_plane = 0 if side == 0 else planes
                    scale = jnp.where(hears_side[side], half, 0.0)
                    span = slice(q * part, (q + 1) * part)
                    az[low_plane, span] = scale * (cond[low_plane, span] + cond[low_plane + 1, span])
                advance_part(k, edge, q)
                if k < FSTEPS - 1:
                    @pl.when(sends_side[1 - side])
                    def _(side=side):
                        halo(k + 1, 1 - side, q).start()

        if k < FSTEPS - 1:
            inner_planes(k)

    total_rows = blocks * cplanes * crows

    def coarse_faces():
        c = unpacked([ext[b, 1] for b in range(blocks)])
        half_c = 0.5 * fine_rate * FSTEPS / 16.0
        row = lax.broadcasted_iota(jnp.int32, (total_rows, LANES), 0)
        col = lax.broadcasted_iota(jnp.int32, (total_rows, LANES), 1)
        cx = jnp.where(row % crows < crows - 1, half_c * (c + pltpu.roll(c, total_rows - 1, 0)), 0.0)
        cy = jnp.where(col < ccols - 1, half_c * (c + pltpu.roll(c, LANES - 1, 1)), 0.0)
        ahead = row + (me - far) * (cplanes * crows)
        valid = (ahead >= 0) & (ahead < (slabs * cplanes - 1) * crows) & (row < total_rows - crows)
        cz = jnp.where(valid, half_c * (c + pltpu.roll(c, total_rows - crows, 0)), 0.0)
        return cx, cy, cz

    def propagate(w, coef):
        cx, cy, cz = coef
        fx = cx * (pltpu.roll(w, total_rows - 1, 0) - w)
        fy = cy * (pltpu.roll(w, LANES - 1, 1) - w)
        fz = cz * (pltpu.roll(w, total_rows - crows, 0) - w)
        div = (fz - pltpu.roll(fz, crows, 0)) + (fx - pltpu.roll(fx, 1, 0)) + (fy - pltpu.roll(fy, 1, 1))
        return w + div

    centre = slice(far * cplanes * crows, (far + 1) * cplanes * crows)

    def start_copy(delta):
        return pltpu.make_async_remote_copy(
            src_ref=first.at[0], dst_ref=first.at[1],
            send_sem=ssend.at[delta - 1], recv_sem=srecv,
            device_id=(tm + delta, me), device_id_type=MESH,
        )

    def pass_token(r):
        @pl.when((tm > 0) & (tm + r < slices))
        def _():
            pl.semaphore_signal(token.at[r], inc=1, device_id=(tm - 1, me), device_id_type=MESH)

    def take_token(r):
        @pl.when(tm + 1 + r < slices)
        def _():
            pl.semaphore_wait(token.at[r], 1)

    def send_start(delta):
        @pl.when(tm == 0)
        def _():
            start_copy(delta).start()

    fine_step(0)
    early_send(offsets)
    if slices > 1:
        pass_token(0)

    fine_step(1)
    for d in offsets:
        @pl.when(inside(d))
        def _(d=d):
            early(-d).wait_recv()
    for b in range(blocks):
        first[0, b] = ext[b, 0]
    for r in range(slices - 2):
        if r == 0:
            take_token(0)
            pass_token(1)
    if slices > 1:
        if slices == 2:
            take_token(0)
        send_start(1)
    coef = coarse_faces()
    coarse_old = propagate(unpacked([first[0, b] for b in range(blocks)]), coef)[centre]
    fine_step(2)
    for r in range(1, slices - 1):
        take_token(r)
        if r + 1 < slices - 1:
            pass_token(r + 1)
        if r < slices - 2:
            send_start(r + 1)
    fine_step(3)
    if slices > 2:
        send_start(slices - 1)

    jump[...] = packed(restrict(field, (FSTEPS,)) - coarse_old)

    def jump_copy(delta, d):
        at = (delta - 1) * blocks
        return pltpu.make_async_remote_copy(
            src_ref=jump, dst_ref=jumps.at[delta - 1, far - d],
            send_sem=jsend.at[at + far + d], recv_sem=jrecv.at[at + far - d],
            device_id=(tm + delta, me + d), device_id_type=MESH,
        )

    routes = [
        (delta, d)
        for delta in range(1, slices)
        for d in sorted(range(-reach(delta), reach(delta) + 1), key=lambda d: -abs(d))
    ]
    for delta, d in routes:
        @pl.when(later(delta) & inside(d))
        def _(delta=delta, d=d):
            jump_copy(delta, d).start()

    @pl.when(tm > 0)
    def _():
        start_copy(1).wait_recv()

    @pl.when(tm == 0)
    def _():
        first[1] = first[0]

    w = unpacked([first[1, b] for b in range(blocks)])
    for delta in range(slices - 1, 0, -1):
        for at, d in routes:
            if at == delta:
                @pl.when((tm >= delta) & inside(d))
                def _(delta=delta, d=d):
                    jump_copy(delta, -d).wait_recv()
        new = propagate(w, coef) + unpacked([jumps[delta - 1, b] for b in range(blocks)])
        w = jnp.where(tm >= delta, new, w)
    change = propagate(w, coef)[centre] - coarse_old

    spread_x = group_matrix((cplanes * rows, cplanes * crows), 1)
    spread_y = group_matrix((LANES, cols), 0)
    spread = dot_right(dot_left(spread_x, change), spread_y)
    stores = []
    for c in range(cplanes):
        piece = spread[c * rows : (c + 1) * rows]
        at = 1 + c * coarsen
        for j in range(coarsen):
            field[FSTEPS, at + j] = field[FSTEPS, at + j] + piece
        store = pltpu.make_async_copy(
            field.at[FSTEPS, pl.ds(at, coarsen)],
            out.at[0, pl.ds(c * coarsen, coarsen)],
            load_sem.at[2 + c],
        )
        store.start()
        stores.append(store)

    for side in range(2):
        @pl.when(sends_side[side])
        def _(side=side):
            for q in range(PARTS):
                halo_c(side, q).wait_send()
            for k in range(FSTEPS):
                for q in range(PARTS):
                    halo(k, side, q).wait_send()
    for d in offsets:
        @pl.when(inside(d))
        def _(d=d):
            early(d).wait_send()
    for delta in range(1, slices):
        @pl.when(tm == 0)
        def _(delta=delta):
            start_copy(delta).wait_send()
    for delta, d in routes:
        @pl.when(later(delta) & inside(d))
        def _(delta=delta, d=d):
            jump_copy(delta, d).wait_send()
    for store in stores:
        store.wait()


def per_device(slices, slabs, states, conductivity):
    _, planes, rows, cols = states.shape
    cplanes, crows = planes // coarsen, rows // coarsen
    pack = LANES // (cols // coarsen)
    packed_rows = cplanes // pack * crows

    def reach(delta):
        return -(-delta // cplanes)

    far = reach(slices)
    blocks = 2 * far + 1
    f32 = jnp.float32
    dma = pltpu.SemaphoreType.DMA
    hops = max(slices - 1, 1)
    return pl.pallas_call(
        functools.partial(kernel, slices, slabs, reach),
        out_shape=jax.ShapeDtypeStruct(states.shape, f32),
        in_specs=[pl.BlockSpec(memory_space=pltpu.HBM)] * 2,
        out_specs=pl.BlockSpec(memory_space=pl.ANY),
        scratch_shapes=[
            pltpu.VMEM((FSTEPS + 1, planes + 2, rows, cols), f32),
            pltpu.VMEM((planes + 2, rows, cols), f32),
            pltpu.VMEM((planes, rows, cols), f32),
            pltpu.VMEM((planes, rows, cols), f32),
            pltpu.VMEM((planes + 1, rows, cols), f32),
            pltpu.VMEM((2, packed_rows, LANES), f32),
            pltpu.VMEM((blocks, 2, packed_rows, LANES), f32),
            pltpu.VMEM((2, blocks, packed_rows, LANES), f32),
            pltpu.VMEM((packed_rows, LANES), f32),
            pltpu.VMEM((hops, blocks, packed_rows, LANES), f32),
            dma((2 + cplanes,)),
            dma((FSTEPS, 2, PARTS)),
            dma((FSTEPS, 2, PARTS)),
            dma((2, PARTS)),
            dma((2, PARTS)),
            dma((blocks,)),
            dma((blocks,)),
            dma((hops,)),
            dma,
            dma((hops * blocks,)),
            dma((hops * blocks,)),
            pltpu.SemaphoreType.REGULAR((hops,)),
        ],
        compiler_params=pltpu.CompilerParams(
            collective_id=0, has_side_effects=True, vmem_limit_bytes=32 * 1024 * 1024
        ),
    )(states, conductivity)


def solution(mesh):
    in_specs = (P("tm", "space", None, None), P("space", None, None))
    out_specs = P("tm", "space", None, None)
    return jax.shard_map(
        functools.partial(per_device, mesh.shape["tm"], mesh.shape["space"]),
        mesh=mesh, in_specs=in_specs, out_specs=out_specs, check_vma=False,
    )
```
